256 devices in a mesh: ctx: 64 (over x, z, core), head: 4 (over y).
Axes of the slice: x: 4, y: 4, z: 8, core: 2. Of those that a mesh axis runs over, the one named last changes fastest.
Arguments:
- queries: bfloat16 [8192, 16, 512], P('ctx', 'head'), may hold values from -5 to 5
- hist_keys: bfloat16 [131072, 16, 128], P('ctx', 'head'), may hold values from -5 to 5
- hist_values: bfloat16 [131072, 16, 128], P('ctx', 'head'), may hold values from -5 to 5
- own_keys: bfloat16 [8192, 16, 128], P('ctx', 'head'), may hold values from -5 to 5
- own_values: bfloat16 [8192, 16, 128], P('ctx', 'head'), may hold values from -5 to 5
- choices: int32 [16, 8192, 3], P('head', 'ctx'), may hold values from 0 to 63, all different within a row; in each aligned block of 128 rows (0 to 127, 128 to 255, ..., all dimensions but the last counted through in order) at most 8 rows name the same one
- positions: int32 [64, 128], P('ctx'), may hold values from 0 to 127, each once within a row
Outputs:
- attended: bfloat16 [8192, 16, 512], P(('ctx', 'head'))
The draws below stay inside these ranges and needn't reach their ends.
Inputs may be any that keep to these rules, and one draw needn't show every extreme that they name: `choices`: the three numbers of a row differ; within the 128 tokens of one device in one group no block is chosen more than 8 times, and some block exactly 8 times. `positions`: each device's row holds each of 0 to 127 once.
All inputs are finite; a program needn't handle non-finite values.
Results may differ from the reference program's by a relative error of at most 0.0047.
Values may be sent and summed in bfloat16 or wider, within the bound.
No kernel may reach another device: no remote copies, remote signals or barrier semaphores. Data moves between devices by JAX's collectives and lax.ppermute only.
A program may use at most 128 MiB of HBM per device.

```python
import math
import jax
import jax.numpy as jnp
import numpy as np
from jax import lax

DH = 128
HPG = 4
GROUPS = 16
BLOCK = 2048
QDEV = 128
NBLK = 64
TOKENS = 8192
KEYS = 131072
CAP = 8


def draw_queries(key, part):
    key = jax.random.fold_in(key, 1)
    first_key = jax.random.fold_in(key, 0)
    shape_full = (TOKENS, GROUPS, HPG * DH)
    values_out = jnp.clip(jax.random.normal(first_key, shape_full, jnp.float32), -5.0, 5.0)
    return values_out.astype(jnp.bfloat16)


def draw_hist_keys(key, part):
    key = jax.random.fold_in(key, 2)
    first_key = jax.random.fold_in(key, 0)
    shape_full = (NBLK, BLOCK, GROUPS, DH)
    values_out = jnp.clip(jax.random.normal(first_key, shape_full, jnp.float32), -5.0, 5.0)
    return values_out.reshape(KEYS, GROUPS, DH).astype(jnp.bfloat16)


def draw_own_keys(key, part):
    key = jax.random.fold_in(key, 3)
    first_key = jax.random.fold_in(key, 0)
    shape_full = (TOKENS, GROUPS, DH)
    values_out = jnp.clip(jax.random.normal(first_key, shape_full, jnp.float32), -5.0, 5.0)
    return values_out.astype(jnp.bfloat16)


def level_of(stream_key, extent, cuts, smallest, top_value):
    gain = 1.0
    for dim, blocks in cuts:
        heights = jax.random.uniform(jax.random.fold_in(jax.random.fold_in(stream_key, 6), dim), (blocks,), jnp.float32, smallest / len(cuts), top_value / len(cuts))
        gain = gain * jnp.repeat(jnp.exp(heights), extent[dim] // blocks).reshape((-1,) + (1,) * (len(extent) - 1 - dim))
    return gain


def shared_out(stream_key, own, number, rows, count, top, bound, lean):
    sequence = jax.random.permutation(stream_key, count)
    crowded, common = portions_of(count, rows * top, bound, lean, True), portions_of(count, rows * top, bound, lean, False)
    places = jnp.arange(count)

    def named(lengths, rotation):
        used = int((lengths > 0).sum())
        fixed = max(1, used // 4)
        moved = fixed + (places - fixed + rotation * (used - fixed)) % max(1, count - fixed)
        return jnp.zeros((count,), jnp.int32).at[sequence[jnp.where(places < fixed, places, moved)]].set(jnp.asarray(lengths, jnp.int32))

    lengths = jnp.where(number % 4 == 0, named(crowded, number // 4), named(common, number - number // 4 - 1))
    mixed = jax.random.permutation(jax.random.fold_in(own, 3), count)
    giver, receiver = mixed[0:count // 2 * 2:2], mixed[1:count // 2 * 2:2]
    room = jnp.minimum(lengths[giver] - 1, bound - lengths[receiver]) // 2
    room = jnp.where((giver == sequence[0]) | (receiver == sequence[0]) | (lengths[receiver] == 0), 0, jnp.maximum(room, 0))
    moved = jax.random.randint(jax.random.fold_in(own, 4), (count // 2,), 0, 1 << 20) % (room + 1)
    lengths = lengths.at[giver].add(-moved).at[receiver].add(moved)
    labels = jnp.searchsorted(jnp.cumsum(lengths), jnp.arange(rows * top), side="right").astype(jnp.int32)
    grid = labels.reshape(top, rows).T
    grid = grid[jax.random.permutation(jax.random.fold_in(own, 1), rows)]
    rotation = jax.random.randint(jax.random.fold_in(own, 2), (rows, 1), 0, top)
    return jnp.take_along_axis(grid, (jnp.arange(top)[None, :] + rotation) % top, axis=1)


def portions_of(amount, total, bound, slope, full):
    weights = [(1 << 20) // math.isqrt(grade ** slope) + 1 for grade in range(1, amount + 1)]
    largest = bound if full else min(bound, max(-(-total // amount), total * weights[0] // sum(weights)))
    least = 1 if total - largest >= amount - 1 else 0
    given, surplus = [largest] + [least] * (amount - 1), total - largest - least * (amount - 1)
    while surplus > 0:
        movable = [i for i in range(1, amount) if given[i] < largest] or [i for i in range(1, amount) if given[i] < bound]
        pool, left = sum([weights[i] for i in movable]), surplus
        for i in movable:
            more = min(bound - given[i], max(1, left * weights[i] // pool), surplus)
            given[i] = given[i] + more
            surplus = surplus - more
    return np.array(given)


def gaussian(own_key, shape, deviation, reach, cuts=(), kind=jnp.bfloat16):
    values = jax.random.normal(own_key, shape, jnp.float32) * deviation
    if len(cuts) > 0:
        values = level_of(own_key, shape, cuts, -0.22, 0.18) * values
    return jnp.clip(values, min=-reach, max=reach).astype(kind)


def setup_inputs(seed: int = 0) -> dict:
    keys = jax.random.split(jax.random.key(seed), 8)
    queries = draw_queries(jax.random.fold_in(keys[7], 71), 0)
    hist_keys = draw_hist_keys(jax.random.fold_in(keys[7], 71), 0)
    hist_values = gaussian(keys[2], (KEYS, GROUPS, DH), 1.0, 5.0, ((0, 64), (1, 4)))
    own_keys = draw_own_keys(jax.random.fold_in(keys[7], 71), 0)
    own_values = gaussian(keys[4], (TOKENS, GROUPS, DH), 1.0, 5.0, ((0, 64), (1, 4)))
    choices_keys = jax.random.split(jax.random.fold_in(keys[5], 1), GROUPS * TOKENS // QDEV)
    choices_turns = jax.random.permutation(jax.random.fold_in(keys[5], 3), GROUPS * TOKENS // QDEV)
    choices = jax.vmap(lambda own, number: shared_out(jax.random.fold_in(keys[5], 2), own, number, QDEV, NBLK, 3, CAP, 2))(choices_keys, choices_turns).reshape((GROUPS, TOKENS, 3))
    positions = jax.vmap(lambda own: jax.random.permutation(own, QDEV))(jax.random.split(keys[6], NBLK)).reshape((NBLK, QDEV)).astype(jnp.int32)
    return {"queries": queries, "hist_keys": hist_keys, "hist_values": hist_values, "own_keys": own_keys, "own_values": own_values, "choices": choices, "positions": positions}


def attend(query_rows, key_rows, value_rows, allowed):
    scores = jnp.dot(query_rows, key_rows.T, preferred_element_type=jnp.float32) * (DH ** -0.5)
    if allowed is not None:
        scores = jnp.where(allowed, scores, -jnp.inf)
    highest = jnp.max(scores, axis=1, keepdims=True)
    weights = jnp.exp(scores - highest)
    denominator = jnp.sum(weights, axis=1, keepdims=True)
    blended = jnp.dot(weights.astype(jnp.bfloat16), value_rows, preferred_element_type=jnp.float32) / denominator
    return blended, (highest + jnp.log(denominator))[:, 0]


def reference(queries, hist_keys, hist_values, own_keys, own_values, choices, positions):
    row_width = HPG * DH
    slot_count = NBLK * CAP
    block_ids = jnp.arange(NBLK, dtype=jnp.int32)
    token_ids = jnp.arange(TOKENS, dtype=jnp.int32)
    sources = token_ids // QDEV
    query_pos = positions.reshape(TOKENS)

    def one_group(group):
        group_queries = lax.dynamic_index_in_dim(queries, group, 1, keepdims=False)
        group_keys = lax.dynamic_index_in_dim(hist_keys, group, 1, keepdims=False).reshape(NBLK, BLOCK, DH)
        group_values = lax.dynamic_index_in_dim(hist_values, group, 1, keepdims=False).reshape(NBLK, BLOCK, DH)
        near_keys = lax.dynamic_index_in_dim(own_keys, group, 1, keepdims=False)
        near_values = lax.dynamic_index_in_dim(own_values, group, 1, keepdims=False)
        chosen = lax.dynamic_index_in_dim(choices, group, 0, keepdims=False).astype(jnp.int32)
        one_hot = (chosen[:, :, None] == block_ids).astype(jnp.int32)
        occupied = jnp.sum(one_hot, axis=1).reshape(NBLK, QDEV, NBLK)
        earlier = (jnp.cumsum(occupied, axis=1) - occupied).reshape(TOKENS, NBLK)
        slot_rank = jnp.sum(one_hot * earlier[:, None, :], axis=2)
        columns = (sources[:, None] * CAP + slot_rank).astype(jnp.int32)
        slot_table = jnp.full((NBLK, slot_count), TOKENS, jnp.int32)
        slot_table = slot_table.at[chosen, columns].set(jnp.broadcast_to(token_ids[:, None], (TOKENS, 3)))
        padded = jnp.concatenate([group_queries, jnp.zeros((1, row_width), group_queries.dtype)], axis=0)

        def remote(block_id):
            query_rows = padded[slot_table[block_id]].reshape(slot_count * HPG, DH)
            blended, log_total = attend(query_rows, group_keys[block_id], group_values[block_id], None)
            return blended.reshape(slot_count, row_width), log_total.reshape(slot_count, HPG)

        far_out, far_lse = lax.map(remote, block_ids)
        back_out = far_out[chosen, columns]
        back_lse = far_lse[chosen, columns]

        def near_part(device):
            first_row = (device * QDEV).astype(jnp.int32)
            query_rows = lax.dynamic_slice_in_dim(group_queries, first_row, QDEV, 0).reshape(QDEV * HPG, DH)
            key_rows = lax.dynamic_slice_in_dim(near_keys, first_row, QDEV, 0)
            value_rows = lax.dynamic_slice_in_dim(near_values, first_row, QDEV, 0)
            local_pos = lax.dynamic_slice_in_dim(query_pos, first_row, QDEV, 0)
            allowed = jnp.repeat(local_pos[None, :] <= local_pos[:, None], HPG, axis=0)
            blended, log_total = attend(query_rows, key_rows, value_rows, allowed)
            return blended.reshape(QDEV, row_width), log_total.reshape(QDEV, HPG)

        own_out, own_lse = lax.map(near_part, block_ids)
        all_lse = jnp.concatenate([own_lse.reshape(TOKENS, 1, HPG), back_lse], axis=1)
        all_out = jnp.concatenate([own_out.reshape(TOKENS, 1, HPG, DH), back_out.reshape(TOKENS, 3, HPG, DH)], axis=1)
        highest = jnp.max(all_lse, axis=1, keepdims=True)
        weights = jnp.exp(all_lse - highest)
        merged = jnp.sum(weights[..., None] * all_out, axis=1) / jnp.sum(weights, axis=1)[..., None]
        return merged.reshape(TOKENS, row_width).astype(jnp.bfloat16)

    result = lax.map(one_group, jnp.arange(GROUPS, dtype=jnp.int32))
    return jnp.transpose(result, (1, 0, 2))
```

```python
import math

import jax
import jax.numpy as jnp
from jax import lax
from jax.experimental import pallas as pl
from jax.experimental.pallas import tpu as pltpu
from jax.sharding import PartitionSpec as P

CHUNKS = 2
LSE_ROWS = 8
VMEM_LIMIT = 56 * 1024 * 1024
TILE_SOURCES = 8


def whole():
    return pl.BlockSpec(memory_space=pltpu.VMEM)


def slot_of(chosen, sources, capacity):
    tokens = chosen.shape[0]
    block_ids = lax.broadcasted_iota(jnp.int32, (tokens, sources), 1)
    hits = [(chosen[:, j : j + 1] == block_ids).astype(jnp.float32) for j in range(3)]
    occupied = (hits[0] + hits[1] + hits[2]).astype(jnp.bfloat16)
    row = lax.broadcasted_iota(jnp.int32, (tokens, tokens), 0)
    column = lax.broadcasted_iota(jnp.int32, (tokens, tokens), 1)
    before = (column < row).astype(jnp.bfloat16)
    earlier = jnp.dot(before, occupied, preferred_element_type=jnp.float32)
    ranks = [jnp.sum(hit * earlier, axis=1, keepdims=True).astype(jnp.int32) for hit in hits]
    return hits, ranks


def slot_hits(chosen, ranks, sources, capacity):
    tokens = chosen.shape[0]
    slot_ids = lax.broadcasted_iota(jnp.int32, (tokens, sources * capacity), 1)
    return [(chosen[:, j : j + 1] * capacity + ranks[j]) == slot_ids for j in range(3)]


def dispatch_kernel(sources, capacity, heads, width, q_ref, choices_ref, *out_refs):
    groups = choices_ref.shape[0]
    per_chunk = groups // len(out_refs)
    row_width = heads * width
    for g in range(groups):
        chosen = choices_ref[g]
        _, ranks = slot_of(chosen, sources, capacity)
        hit = slot_hits(chosen, ranks, sources, capacity)
        pick = (hit[0] | hit[1] | hit[2]).astype(jnp.float32).T.astype(jnp.bfloat16)
        rows = q_ref[:, g * row_width : (g + 1) * row_width]
        filled = jnp.dot(pick, rows, preferred_element_type=jnp.float32)
        filled = filled.reshape(sources, capacity, row_width)
        by_head = [filled[:, :, h * width : (h + 1) * width] for h in range(heads)]
        out_refs[g // per_chunk][:, g % per_chunk] = jnp.concatenate(by_head, axis=1).astype(
            jnp.bfloat16
        )


def far_kernel(first_group, scale, last, q_ref, k_ref, v_ref, *refs):
    if last:
        lse_in_ref, out_ref, lse_ref, wide_ref = refs
    else:
        out_ref, lse_ref, wide_ref = refs
    g = pl.program_id(0)
    sources, _, per_source, width = q_ref.shape
    keys = k_ref.shape[0]
    wide_ref[:, :width] = v_ref[...]
    wide_ref[:, width:] = jnp.ones((keys, width), jnp.bfloat16)

    @pl.when(g == 0)
    def _():
        lse_ref[...] = lse_in_ref[...] if last else jnp.zeros_like(lse_ref)

    rows = TILE_SOURCES * per_source
    fold = scale * math.log2(math.e)

    def tile(start):
        q = q_ref[pl.ds(start, TILE_SOURCES), 0].reshape(rows, width)
        scores = lax.dot_general(
            q, k_ref[...], (((1,), (1,)), ((), ())), preferred_element_type=jnp.float32
        )
        highest = jnp.max(scores, axis=1, keepdims=True)
        weights = jnp.exp2((scores - highest) * fold).astype(jnp.bfloat16)
        both = jnp.dot(weights, wide_ref[...], preferred_element_type=jnp.float32)
        total = both[:, width:]
        blended = both[:, :width] / total
        lse = highest * scale + jnp.log(total)
        return blended, lse

    lane = lax.broadcasted_iota(jnp.int32, (TILE_SOURCES, per_source, width), 2)
    index = lax.broadcasted_iota(jnp.int32, (TILE_SOURCES, per_source, width), 1)
    mine = lane == index + (first_group + g) * per_source

    def step(i, carry):
        starts = [pl.multiple_of((2 * i + n) * TILE_SOURCES, TILE_SOURCES) for n in range(2)]
        results = [tile(start) for start in starts]
        for start, (blended, lse) in zip(starts, results):
            at = pl.ds(start, TILE_SOURCES)
            out_ref[at, pl.ds(pl.multiple_of(g * per_source, per_source), per_source), :] = (
                blended.reshape(TILE_SOURCES, per_source, width).astype(jnp.bfloat16)
            )
            spread = jnp.where(mine, lse.reshape(TILE_SOURCES, per_source, width), 0.0)
            lse_ref[at, :] += jnp.sum(spread, axis=1)
        return carry

    lax.fori_loop(0, sources // (2 * TILE_SOURCES), step, 0)

    if last:

        @pl.when(g == pl.num_programs(0) - 1)
        def _():
            table = lse_ref[...]
            coarse = table.astype(jnp.bfloat16).astype(jnp.float32)
            fine = table - coarse
            rest = jnp.zeros((sources, LSE_ROWS - 2, width), jnp.float32)
            extra = jnp.concatenate([coarse[:, None, :], fine[:, None, :], rest], axis=1)
            out_ref[:, pl.num_programs(0) * per_source :, :] = extra.astype(jnp.bfloat16)


def near_kernel(sources, capacity, heads, width, scale, q_ref, k_ref, v_ref, choices_ref,
                row_pos_ref, col_pos_ref, out_ref, lse_ref, pick_ref, block_ref, rank_ref):
    groups, tokens, _ = choices_ref.shape
    allowed = row_pos_ref[...] <= col_pos_ref[...]
    for g in range(groups):
        chosen = choices_ref[g]
        hits, ranks = slot_of(chosen, sources, capacity)
        slots = slot_hits(chosen, ranks, sources, capacity)
        lane = lax.broadcasted_iota(jnp.int32, (tokens, heads * groups * capacity), 1)
        for j in range(3):
            at = slice(j * tokens, (j + 1) * tokens)
            pick_ref[g, at] = slots[j].astype(jnp.float32).astype(jnp.bfloat16)
            block_ref[g, at] = hits[j].astype(jnp.bfloat16)
            in_group = (lane >= g * heads * capacity) & (lane < (g + 1) * heads * capacity)
            here = in_group & (lane % capacity == ranks[j])
            rank_ref[g, at] = here.astype(jnp.float32).astype(jnp.bfloat16)
        keys = k_ref[:, g * width : (g + 1) * width]
        values = v_ref[:, g * width : (g + 1) * width]
        for h in range(heads):
            at = slice((g * heads + h) * width, (g * heads + h + 1) * width)
            scores = lax.dot_general(
                q_ref[:, at], keys, (((1,), (1,)), ((), ())), preferred_element_type=jnp.float32
            )
            scores = jnp.where(allowed, scores * scale, -jnp.inf)
            highest = jnp.max(scores, axis=1, keepdims=True)
            weights = jnp.exp(scores - highest)
            total = jnp.sum(weights, axis=1, keepdims=True)
            blended = jnp.dot(
                weights.astype(jnp.bfloat16), values, preferred_element_type=jnp.float32
            )
            out_ref[:, at] = blended / total
            lse_ref[:, at] = jnp.broadcast_to(highest + jnp.log(total), (tokens, width))


def merge_kernel(capacity, heads, width, near_ref, near_lse_ref, pick_ref, block_ref, rank_ref,
                 *refs):
    back_refs, out_ref = refs[:-1], refs[-1]
    groups = pick_ref.shape[0]
    per_chunk = groups // len(back_refs)
    sources = back_refs[0].shape[0]
    tokens = near_ref.shape[0]
    per_source = heads * capacity
    row_width = heads * width
    extra = back_refs[-1][:, per_chunk * per_source :, :].astype(jnp.float32)
    coarse = extra[:, 0, :].astype(jnp.bfloat16)
    fine = extra[:, 1, :].astype(jnp.bfloat16)
    lane = lax.broadcasted_iota(jnp.int32, (groups * per_source, row_width), 0)
    column = lax.broadcasted_iota(jnp.int32, (groups * per_source, row_width), 1)
    spread = ((lane // capacity) % heads == column // width).astype(jnp.float32)
    spread = spread.astype(jnp.bfloat16)
    for g in range(groups):
        back_ref = back_refs[g // per_chunk]
        first = (g % per_chunk) * per_source
        rows = back_ref[:, first : first + per_source, :].astype(jnp.float32)
        by_head = [
            rows[:, h * capacity : (h + 1) * capacity, :].reshape(sources * capacity, width)
            for h in range(heads)
        ]
        table = jnp.concatenate(by_head, axis=1).astype(jnp.bfloat16)
        got = jnp.dot(pick_ref[g], table, preferred_element_type=jnp.float32)
        lse = jnp.zeros((3 * tokens, row_width), jnp.float32)
        for part in (coarse, fine):
            picked = jnp.dot(block_ref[g], part, preferred_element_type=jnp.float32)
            picked = picked.astype(jnp.bfloat16) * rank_ref[g]
            lse += jnp.dot(picked, spread, preferred_element_type=jnp.float32)
        at = slice(g * row_width, (g + 1) * row_width)
        all_lse = [near_lse_ref[:, at]] + [lse[j * tokens : (j + 1) * tokens] for j in range(3)]
        all_out = [near_ref[:, at]] + [got[j * tokens : (j + 1) * tokens] for j in range(3)]
        highest = all_lse[0]
        for item in all_lse[1:]:
            highest = jnp.maximum(highest, item)
        top = jnp.zeros((tokens, row_width), jnp.float32)
        bottom = jnp.zeros((tokens, row_width), jnp.float32)
        for item, part in zip(all_lse, all_out):
            weight = jnp.exp(item - highest)
            top += weight * part
            bottom += weight
        out_ref[g] = (top / bottom).astype(jnp.bfloat16)


def local(queries, hist_keys, hist_values, own_keys, own_values, choices, positions):
    sources = lax.axis_size("ctx")
    tokens, groups, row_width = queries.shape
    keys, _, width = hist_keys.shape
    heads = row_width // width
    capacity = 4 * tokens // sources
    per_source = heads * capacity
    scale = width ** (-0.5)
    per_chunk = groups // CHUNKS
    params = pltpu.CompilerParams(vmem_limit_bytes=VMEM_LIMIT)
    bf16, f32 = jnp.bfloat16, jnp.float32

    flat_queries = queries.reshape(tokens, groups * row_width)
    outbound = pl.pallas_call(
        lambda *refs: dispatch_kernel(sources, capacity, heads, width, *refs),
        out_shape=[jax.ShapeDtypeStruct((sources, per_chunk, per_source, width), bf16)] * CHUNKS,
        in_specs=[whole()] * 2,
        out_specs=[whole()] * CHUNKS,
        compiler_params=params,
        name="dispatch",
    )(flat_queries, choices)
    received = [lax.all_to_all(item, "ctx", 0, 0, tiled=True) for item in outbound]

    flat_keys = hist_keys.reshape(keys, groups * width)
    flat_values = hist_values.reshape(keys, groups * width)

    def far(chunk, lse_table):
        last = chunk == CHUNKS - 1
        first_group = chunk * per_chunk
        rows = per_chunk * per_source + (LSE_ROWS if last else 0)
        work = per_chunk * sources * per_source * keys
        return pl.pallas_call(
            lambda *refs: far_kernel(first_group, scale, last, *refs),
            grid=(per_chunk,),
            in_specs=[
                pl.BlockSpec((sources, 1, per_source, width), lambda g: (0, g, 0, 0)),
                pl.BlockSpec((keys, width), lambda g: (0, first_group + g)),
                pl.BlockSpec((keys, width), lambda g: (0, first_group + g)),
            ]
            + ([pl.BlockSpec((sources, groups * per_source), lambda g: (0, 0))] if last else []),
            out_specs=[
                pl.BlockSpec((sources, rows, width), lambda g: (0, 0, 0)),
                pl.BlockSpec((sources, groups * per_source), lambda g: (0, 0)),
            ],
            out_shape=[
                jax.ShapeDtypeStruct((sources, rows, width), bf16),
                jax.ShapeDtypeStruct((sources, groups * per_source), f32),
            ],
            scratch_shapes=[pltpu.VMEM((keys, 2 * width), bf16)],
            compiler_params=params,
            cost_estimate=pl.CostEstimate(
                flops=6 * work * width, transcendentals=work, bytes_accessed=4 * work // keys * width
            ),
            name="far",
        )(received[chunk], flat_keys, flat_values, *((lse_table,) if last else ()))

    back = []
    lse_table = jnp.zeros((sources, groups * per_source), f32)
    for chunk in range(CHUNKS):
        out, lse_table = far(chunk, lse_table)
        back.append(lax.all_to_all(out, "ctx", 0, 0, tiled=True))

    flat = (tokens, groups * row_width)
    near = pl.pallas_call(
        lambda *refs: near_kernel(sources, capacity, heads, width, scale, *refs),
        out_shape=[
            jax.ShapeDtypeStruct(flat, f32),
            jax.ShapeDtypeStruct(flat, f32),
            jax.ShapeDtypeStruct((groups, 3 * tokens, sources * capacity), bf16),
            jax.ShapeDtypeStruct((groups, 3 * tokens, sources), bf16),
            jax.ShapeDtypeStruct((groups, 3 * tokens, groups * per_source), bf16),
        ],
        in_specs=[whole()] * 6,
        out_specs=[whole()] * 5,
        compiler_params=params,
        cost_estimate=pl.CostEstimate(
            flops=4 * tokens * tokens * groups * row_width,
            transcendentals=tokens * tokens * groups * heads,
            bytes_accessed=16 * tokens * groups * row_width,
        ),
        name="near",
    )(
        flat_queries,
        own_keys.reshape(tokens, groups * width),
        own_values.reshape(tokens, groups * width),
        choices,
        positions,
        positions.reshape(tokens, 1),
    )

    merged = pl.pallas_call(
        lambda *refs: merge_kernel(capacity, heads, width, *refs),
        out_shape=jax.ShapeDtypeStruct((groups, tokens, row_width), bf16),
        in_specs=[whole()] * (5 + CHUNKS),
        out_specs=whole(),
        compiler_params=params,
        name="merge",
    )(*near, *back)
    merged = jnp.transpose(merged, (1, 0, 2))
    return lax.all_to_all(merged, "head", split_axis=0, concat_axis=1, tiled=True)


def solution(mesh):
    in_specs = (
        P("ctx", "head", None),
        P("ctx", "head", None),
        P("ctx", "head", None),
        P("ctx", "head", None),
        P("ctx", "head", None),
        P("head", "ctx", None),
        P("ctx", None),
    )
    out_specs = P(("ctx", "head"), None, None)
    return jax.shard_map(local, mesh=mesh, in_specs=in_specs, out_specs=out_specs, check_vma=False)
```

```python
import math

import jax
import jax.numpy as jnp
from jax import lax
from jax.experimental import pallas as pl
from jax.experimental.pallas import tpu as pltpu
from jax.sharding import PartitionSpec as P

SPLIT = (3, 1)
LSE_ROWS = 8
KEY_CHUNK = 256
TILES = 4
WIDE_LIMIT = 60 * 1024 * 1024
SMALL_LIMIT = 24 * 1024 * 1024


def whole():
    return pl.BlockSpec(memory_space=pltpu.VMEM)


def columns_of(choices_ref):
    count, groups, tokens = choices_ref.shape
    rows = choices_ref[...].astype(jnp.float32).reshape(count * groups, tokens)
    pad = jnp.zeros((tokens - count * groups, tokens), jnp.float32)
    columns = jnp.concatenate([rows, pad], axis=0).T.astype(jnp.int32)
    return [[columns[:, j * groups + g : j * groups + g + 1] for j in range(count)] for g in range(groups)]


def ranks_of(chosen, sources):
    tokens = chosen[0].shape[0]
    block_ids = lax.broadcasted_iota(jnp.int32, (tokens, sources), 1)
    hits = [(item == block_ids).astype(jnp.float32) for item in chosen]
    occupied = (hits[0] + hits[1] + hits[2]).astype(jnp.bfloat16)
    row = lax.broadcasted_iota(jnp.int32, (tokens, tokens), 0)
    column = lax.broadcasted_iota(jnp.int32, (tokens, tokens), 1)
    before = (column < row).astype(jnp.bfloat16)
    earlier = jnp.dot(before, occupied, preferred_element_type=jnp.float32)
    return [jnp.sum(hit * earlier, axis=1, keepdims=True).astype(jnp.int32) for hit in hits]


def dispatch_kernel(first, sources, capacity, heads, width, q_ref, choices_ref, out_ref):
    tokens = choices_ref.shape[2]
    row_width = heads * width
    chosen = columns_of(choices_ref)
    slot_ids = lax.broadcasted_iota(jnp.int32, (tokens, sources * capacity), 1)
    for i in range(out_ref.shape[1]):
        g = first + i
        hit = None
        for block, rank in zip(chosen[g], ranks_of(chosen[g], sources)):
            mine = block * capacity + rank == slot_ids
            hit = mine if hit is None else hit | mine
        pick = hit.astype(jnp.float32).T.astype(jnp.bfloat16)
        rows = q_ref[:, g * row_width : (g + 1) * row_width]
        filled = jnp.dot(pick, rows, preferred_element_type=jnp.float32)
        filled = filled.reshape(sources, capacity, row_width)
        by_head = [filled[:, :, h * width : (h + 1) * width] for h in range(heads)]
        out_ref[:, i] = jnp.concatenate(by_head, axis=1).astype(jnp.bfloat16)


def far_kernel(first, last, scale, q_ref, k_ref, v_ref, *refs):
    if last:
        _, lse_in_ref, out_ref, lse_ref, wide_ref = refs
    else:
        out_ref, lse_ref, wide_ref = refs
    g = pl.program_id(0)
    sources, _, per_source, width = q_ref.shape
    keys = k_ref.shape[0]
    wide_ref[:, :width] = v_ref[...]
    wide_ref[:, width:] = jnp.ones((keys, width), jnp.bfloat16)
    fold = scale * math.log2(math.e)

    @pl.when(g == 0)
    def _():
        lse_ref[...] = lse_in_ref[...] if last else jnp.zeros_like(lse_ref)

    deep = sources // TILES
    rows = deep * per_source
    shape = (deep, per_source, width)
    lane = lax.broadcasted_iota(jnp.int32, shape, 2)
    index = lax.broadcasted_iota(jnp.int32, shape, 1)
    mine = lane == index + (first + g) * per_source
    for tile in range(TILES):
        here = slice(tile * deep, (tile + 1) * deep)
        q = q_ref[here, 0].reshape(rows, width)
        highest = None
        for start in range(0, keys, KEY_CHUNK):
            scores = lax.dot_general(
                q,
                k_ref[start : start + KEY_CHUNK],
                (((1,), (1,)), ((), ())),
                preferred_element_type=jnp.float32,
            )
            top = jnp.max(scores, axis=1, keepdims=True)
            top = top if highest is None else jnp.maximum(highest, top)
            weights = jnp.exp2((scores - top) * fold).astype(jnp.bfloat16)
            part = jnp.dot(
                weights, wide_ref[start : start + KEY_CHUNK], preferred_element_type=jnp.float32
            )
            both = part if highest is None else both * jnp.exp2((highest - top) * fold) + part
            highest = top
        total = both[:, width:]
        blended = both[:, :width] / total
        lse = (highest * scale + jnp.log(total)).reshape(shape)
        out_ref[here, :per_source, :] = blended.astype(jnp.bfloat16).reshape(shape)
        lse_ref[here] += jnp.sum(jnp.where(mine, lse, 0.0), axis=1)

    if last:
        table = lse_ref[...]
        coarse = table.astype(jnp.bfloat16).astype(jnp.float32)
        rest = jnp.zeros((sources, LSE_ROWS - 2, width), jnp.float32)
        extra = jnp.concatenate([coarse[:, None, :], (table - coarse)[:, None, :], rest], axis=1)
        out_ref[:, per_source:, :] = extra.astype(jnp.bfloat16)


def near_kernel(sources, capacity, heads, width, scale, q_ref, k_ref, v_ref, choices_ref,
                row_pos_ref, col_pos_ref, out_ref, lse_ref, slot_ref):
    groups, tokens = choices_ref.shape[1:]
    allowed = row_pos_ref[...] <= col_pos_ref[...]
    chosen = columns_of(choices_ref)
    for g in range(groups):
        for j, (block, rank) in enumerate(zip(chosen[g], ranks_of(chosen[g], sources))):
            slot_ref[:, 3 * g + j : 3 * g + j + 1] = block * capacity + rank
        keys = k_ref[:, g * width : (g + 1) * width]
        values = v_ref[:, g * width : (g + 1) * width]
        for h in range(heads):
            at = slice((g * heads + h) * width, (g * heads + h + 1) * width)
            scores = lax.dot_general(
                q_ref[:, at], keys, (((1,), (1,)), ((), ())), preferred_element_type=jnp.float32
            )
            scores = jnp.where(allowed, scores * scale, -jnp.inf)
            highest = jnp.max(scores, axis=1, keepdims=True)
            weights = jnp.exp(scores - highest)
            total = jnp.sum(weights, axis=1, keepdims=True)
            blended = jnp.dot(
                weights.astype(jnp.bfloat16), values, preferred_element_type=jnp.float32
            )
            out_ref[:, at] = blended / total
            lse_ref[:, g * heads + h : g * heads + h + 1] = highest + jnp.log(total)


def merge_kernel(capacity, heads, width, place_ref, near_ref, near_lse_ref, slot_ref, back_ref, *refs):
    out_refs, row_ref = refs[:-1], refs[-1]
    tokens = near_ref.shape[0]
    sources = back_ref.shape[0]
    per_source = heads * capacity
    groups = out_refs[0].shape[0]
    lanes = groups * per_source
    row_width = heads * width
    quarter = tokens // len(out_refs)
    extra = back_ref[:, lanes:, :].astype(jnp.float32)
    coarse = extra[:, 0, :].astype(jnp.bfloat16)
    fine = extra[:, 1, :].astype(jnp.bfloat16)
    lane = lax.broadcasted_iota(jnp.int32, (lanes, row_width), 0)
    column = lax.broadcasted_iota(jnp.int32, (lanes, row_width), 1)
    spread = ((lane // capacity) % heads == column // width).astype(jnp.float32)
    spread = spread.astype(jnp.bfloat16)
    block_ids = lax.broadcasted_iota(jnp.int32, (tokens, sources), 1)
    slot_ids = lax.broadcasted_iota(jnp.int32, (tokens, sources * capacity), 1)
    lane_ids = lax.broadcasted_iota(jnp.int32, (tokens, lanes), 1)
    for g in range(groups):
        slots = [slot_ref[:, 3 * g + j : 3 * g + j + 1] for j in range(3)]
        pick = jnp.concatenate([(slot == slot_ids).astype(jnp.float32) for slot in slots], axis=0)
        block = jnp.concatenate(
            [(slot // capacity == block_ids).astype(jnp.float32) for slot in slots], axis=0
        ).astype(jnp.bfloat16)
        in_group = lane_ids // per_source == g
        rank = jnp.concatenate(
            [
                (in_group & (lane_ids % capacity == slot % capacity)).astype(jnp.float32)
                for slot in slots
            ],
            axis=0,
        )
        rows = back_ref[:, g * per_source : (g + 1) * per_source, :].astype(jnp.float32)
        by_head = [
            rows[:, h * capacity : (h + 1) * capacity, :].reshape(sources * capacity, width)
            for h in range(heads)
        ]
        table = jnp.concatenate(by_head, axis=1).astype(jnp.bfloat16)
        got = jnp.dot(pick.astype(jnp.bfloat16), table, preferred_element_type=jnp.float32)
        lse = jnp.zeros((3 * tokens, row_width), jnp.float32)
        for part in (coarse, fine):
            picked = jnp.dot(block, part, preferred_element_type=jnp.float32)
            picked = (picked * rank).astype(jnp.bfloat16)
            lse += jnp.dot(picked, spread, preferred_element_type=jnp.float32)
        near_lse = jnp.concatenate(
            [
                jnp.broadcast_to(near_lse_ref[:, k : k + 1], (tokens, width))
                for k in range(g * heads, (g + 1) * heads)
            ],
            axis=1,
        )
        at = slice(g * row_width, (g + 1) * row_width)
        all_lse = [near_lse] + [lse[j * tokens : (j + 1) * tokens] for j in range(3)]
        all_out = [near_ref[:, at]] + [got[j * tokens : (j + 1) * tokens] for j in range(3)]
        highest = all_lse[0]
        for item in all_lse[1:]:
            highest = jnp.maximum(highest, item)
        top = jnp.zeros((tokens, row_width), jnp.float32)
        bottom = jnp.zeros((tokens, row_width), jnp.float32)
        for item, part in zip(all_lse, all_out):
            weight = jnp.exp(item - highest)
            top += weight * part
            bottom += weight
        row_ref[...] = top / bottom
        for step, out_ref in enumerate(out_refs):
            target = lax.rem(place_ref[0] + step, len(out_refs))
            start = pl.multiple_of(target * quarter, quarter)
            out_ref[g] = row_ref[pl.ds(start, quarter)].astype(jnp.bfloat16)


def assemble_kernel(place_ref, *refs):
    piece_refs, out_ref = refs[:-1], refs[-1]
    count = len(piece_refs)
    for step, piece_ref in enumerate(piece_refs):
        out_ref[lax.rem(place_ref[0] + count - step, count)] = piece_ref[...]


def local(queries, hist_keys, hist_values, own_keys, own_values, choices, positions):
    sources = lax.axis_size("ctx")
    members = lax.axis_size("head")
    tokens, groups, row_width = queries.shape
    keys, _, width = hist_keys.shape
    heads = row_width // width
    capacity = 4 * tokens // sources
    per_source = heads * capacity
    scale = width ** (-0.5)
    quarter = tokens // members
    bf16, f32 = jnp.bfloat16, jnp.float32
    smem = pl.BlockSpec(memory_space=pltpu.SMEM)

    params = pltpu.CompilerParams(vmem_limit_bytes=WIDE_LIMIT)
    small = pltpu.CompilerParams(vmem_limit_bytes=SMALL_LIMIT)

    flat_queries = queries.reshape(tokens, groups * row_width)
    turned = jnp.transpose(choices, (2, 0, 1))

    def dispatch(first, count):
        return pl.pallas_call(
            lambda *refs: dispatch_kernel(first, sources, capacity, heads, width, *refs),
            out_shape=jax.ShapeDtypeStruct((sources, count, per_source, width), bf16),
            in_specs=[whole()] * 2,
            out_specs=whole(),
            compiler_params=small,
            cost_estimate=pl.CostEstimate(
                flops=2 * count * sources * capacity * tokens * row_width,
                transcendentals=0,
                bytes_accessed=2 * (count * sources * capacity + tokens * groups) * row_width,
            ),
            name="dispatch",
        )(flat_queries, turned)

    flat_keys = hist_keys.reshape(keys, groups * width)
    flat_values = hist_values.reshape(keys, groups * width)
    sent = [dispatch(0, SPLIT[0]), dispatch(SPLIT[0], SPLIT[1])]
    sent[1], flat_keys, flat_values = lax.optimization_barrier((sent[1], flat_keys, flat_values))
    received = [lax.all_to_all(item, "ctx", 0, 0, tiled=True) for item in sent]

    def far(part, *before):
        last = part == 1
        first = SPLIT[0] if last else 0
        out_rows = groups * per_source + LSE_ROWS
        work = SPLIT[part] * sources * per_source * keys
        extra_specs = [
            pl.BlockSpec(memory_space=pl.ANY),
            pl.BlockSpec((sources, groups * per_source), lambda g: (0, 0)),
        ]
        if last:
            tail = pl.Element(per_source + LSE_ROWS)
            block = (pl.Element(sources), tail, pl.Element(width))
            out_spec = pl.BlockSpec(block, lambda g: (0, first * per_source, 0))
        else:
            out_spec = pl.BlockSpec((sources, per_source, width), lambda g: (0, g, 0))
        return pl.pallas_call(
            lambda *refs: far_kernel(first, last, scale, *refs),
            grid=(SPLIT[part],),
            in_specs=[
                pl.BlockSpec((sources, 1, per_source, width), lambda g: (0, g, 0, 0)),
                pl.BlockSpec((keys, width), lambda g: (0, first + g)),
                pl.BlockSpec((keys, width), lambda g: (0, first + g)),
            ]
            + (extra_specs if last else []),
            out_specs=[
                out_spec,
                pl.BlockSpec((sources, groups * per_source), lambda g: (0, 0)),
            ],
            out_shape=[
                jax.ShapeDtypeStruct((sources, out_rows, width), bf16),
                jax.ShapeDtypeStruct((sources, groups * per_source), f32),
            ],
            scratch_shapes=[pltpu.VMEM((keys, 2 * width), bf16)],
            input_output_aliases={3: 0} if last else {},
            compiler_params=params,
            cost_estimate=pl.CostEstimate(
                flops=6 * work * width, transcendentals=work, bytes_accessed=4 * work // keys * width
            ),
            name="far",
        )(received[part], flat_keys, flat_values, *before)

    parts, _ = far(1, *far(0))
    back = lax.all_to_all(parts, "ctx", 0, 0, tiled=True)

    near = pl.pallas_call(
        lambda *refs: near_kernel(sources, capacity, heads, width, scale, *refs),
        out_shape=[
            jax.ShapeDtypeStruct((tokens, groups * row_width), f32),
            jax.ShapeDtypeStruct((tokens, width), f32),
            jax.ShapeDtypeStruct((tokens, width), jnp.int32),
        ],
        in_specs=[whole()] * 6,
        out_specs=[whole()] * 3,
        compiler_params=params,
        cost_estimate=pl.CostEstimate(
            flops=4 * tokens * tokens * groups * row_width,
            transcendentals=tokens * tokens * groups * heads,
            bytes_accessed=16 * tokens * groups * row_width,
        ),
        name="near",
    )(
        flat_queries,
        own_keys.reshape(tokens, groups * width),
        own_values.reshape(tokens, groups * width),
        turned,
        positions,
        positions.reshape(tokens, 1),
    )

    place = lax.axis_index("head").astype(jnp.int32).reshape(1)
    made = pl.pallas_call(
        lambda *refs: merge_kernel(capacity, heads, width, *refs),
        out_shape=[jax.ShapeDtypeStruct((groups, quarter, row_width), bf16)] * members,
        in_specs=[smem] + [whole()] * 4,
        out_specs=[whole()] * members,
        scratch_shapes=[pltpu.VMEM((tokens, row_width), f32)],
        compiler_params=small,
        name="merge",
    )(place, *near, back)
    pieces = []
    for step, item in enumerate(made):
        pairs = [(i, (i + step) % members) for i in range(members)]
        pieces.append(lax.ppermute(item, "head", pairs) if step else item)
    joined = pl.pallas_call(
        assemble_kernel,
        out_shape=jax.ShapeDtypeStruct((members, groups, quarter, row_width), bf16),
        in_specs=[smem] + [whole()] * len(pieces),
        out_specs=whole(),
        compiler_params=small,
        name="assemble",
    )(place, *pieces)
    joined = joined.reshape(members * groups, quarter, row_width)
    return jnp.transpose(joined, (1, 0, 2))


def solution(mesh):
    in_specs = (
        P("ctx", "head", None),
        P("ctx", "head", None),
        P("ctx", "head", None),
        P("ctx", "head", None),
        P("ctx", "head", None),
        P("head", "ctx", None),
        P("ctx", None),
    )
    out_specs = P(("ctx", "head"), None, None)
    return jax.shard_map(local, mesh=mesh, in_specs=in_specs, out_specs=out_specs, check_vma=False)
```

```python
import math

import jax
import jax.numpy as jnp
from jax import lax
from jax.experimental import pallas as pl
from jax.experimental.pallas import tpu as pltpu
from jax.sharding import PartitionSpec as P

PARTS = ((0, 2), (2, 2))
LSE_ROWS = 8
KEY_CHUNK = 256
TILES = 4
ORDER = (2, 1, 3)
WIDE_LIMIT = 60 * 1024 * 1024
SMALL_LIMIT = 24 * 1024 * 1024


def whole():
    return pl.BlockSpec(memory_space=pltpu.VMEM)


def columns_of(choices_ref):
    count, groups, tokens = choices_ref.shape
    rows = choices_ref[...].astype(jnp.float32).reshape(count * groups, tokens)
    pad = jnp.zeros((tokens - count * groups, tokens), jnp.float32)
    columns = jnp.concatenate([rows, pad], axis=0).T.astype(jnp.int32)
    return [[columns[:, j * groups + g : j * groups + g + 1] for j in range(count)] for g in range(groups)]


def ranks_of(chosen, sources):
    tokens = chosen[0].shape[0]
    block_ids = lax.broadcasted_iota(jnp.int32, (tokens, sources), 1)
    hits = [(item == block_ids).astype(jnp.float32) for item in chosen]
    occupied = (hits[0] + hits[1] + hits[2]).astype(jnp.bfloat16)
    row = lax.broadcasted_iota(jnp.int32, (tokens, tokens), 0)
    column = lax.broadcasted_iota(jnp.int32, (tokens, tokens), 1)
    before = (column < row).astype(jnp.bfloat16)
    earlier = jnp.dot(before, occupied, preferred_element_type=jnp.float32)
    return [jnp.sum(hit * earlier, axis=1, keepdims=True).astype(jnp.int32) for hit in hits]


def fill_slots(picked, rows, sources, capacity, heads, width):
    pick = picked.astype(jnp.float32).T.astype(jnp.bfloat16)
    filled = jnp.dot(pick, rows, preferred_element_type=jnp.float32)
    filled = filled.reshape(sources, capacity, heads * width)
    by_head = [filled[:, :, h * width : (h + 1) * width] for h in range(heads)]
    return jnp.concatenate(by_head, axis=1).astype(jnp.bfloat16)


def dispatch_kernel(first, sources, capacity, heads, width, q_ref, choices_ref, out_ref):
    tokens = choices_ref.shape[2]
    row_width = heads * width
    chosen = columns_of(choices_ref)
    slot_ids = lax.broadcasted_iota(jnp.int32, (tokens, sources * capacity), 1)
    for i in range(out_ref.shape[1]):
        g = first + i
        hit = None
        for block, rank in zip(chosen[g], ranks_of(chosen[g], sources)):
            mine = block * capacity + rank == slot_ids
            hit = mine if hit is None else hit | mine
        rows = q_ref[:, g * row_width : (g + 1) * row_width]
        out_ref[:, i] = fill_slots(hit, rows, sources, capacity, heads, width)


def far_group(scale, slot, q_ref, k_ref, v_ref, out_ref, lse_ref, wide_ref):
    sources, _, per_source, width = q_ref.shape
    keys = k_ref.shape[0]
    wide_ref[:, :width] = v_ref[...]
    wide_ref[:, width:] = jnp.ones((keys, width), jnp.bfloat16)
    fold = scale * math.log2(math.e)
    deep = sources // TILES
    rows = deep * per_source
    shape = (deep, per_source, width)
    lane = lax.broadcasted_iota(jnp.int32, shape, 2)
    index = lax.broadcasted_iota(jnp.int32, shape, 1)
    mine = lane == index + slot * per_source
    for tile in range(TILES):
        here = slice(tile * deep, (tile + 1) * deep)
        q = q_ref[here, 0].reshape(rows, width)
        highest = None
        for start in range(0, keys, KEY_CHUNK):
            scores = lax.dot_general(
                q,
                k_ref[start : start + KEY_CHUNK],
                (((1,), (1,)), ((), ())),
                preferred_element_type=jnp.float32,
            )
            top = jnp.max(scores, axis=1, keepdims=True)
            top = top if highest is None else jnp.maximum(highest, top)
            weights = jnp.exp2((scores - top) * fold).astype(jnp.bfloat16)
            part = jnp.dot(
                weights, wide_ref[start : start + KEY_CHUNK], preferred_element_type=jnp.float32
            )
            both = part if highest is None else both * jnp.exp2((highest - top) * fold) + part
            highest = top
        total = both[:, width:]
        blended = both[:, :width] / total
        lse = (highest * scale + jnp.log(total)).reshape(shape)
        out_ref[here] = blended.astype(jnp.bfloat16).reshape(shape)
        lse_ref[here] += jnp.sum(jnp.where(mine, lse, 0.0), axis=1)


def far_kernel(scale, groups, q_ref, k_ref, v_ref, out_ref, lse_ref, wide_ref):
    g = pl.program_id(0)
    sources, width = q_ref.shape[0], k_ref.shape[1]

    @pl.when(g == 0)
    def _():
        lse_ref[...] = jnp.zeros_like(lse_ref)

    @pl.when(g < groups)
    def _():
        far_group(scale, g, q_ref, k_ref, v_ref, out_ref, lse_ref, wide_ref)

    @pl.when(g == groups)
    def _():
        table = lse_ref[...]
        coarse = table.astype(jnp.bfloat16).astype(jnp.float32)
        rest = jnp.zeros((sources, out_ref.shape[1] - 2, width), jnp.float32)
        extra = jnp.concatenate([coarse[:, None, :], (table - coarse)[:, None, :], rest], axis=1)
        out_ref[...] = extra.astype(jnp.bfloat16)


def near_kernel(sources, capacity, heads, width, scale, q_ref, k_ref, v_ref, choices_ref,
                row_pos_ref, col_pos_ref, out_ref):
    groups, tokens = choices_ref.shape[1:]
    allowed = row_pos_ref[...] <= col_pos_ref[...]
    chosen = columns_of(choices_ref)
    for g in range(groups):
        for j, (block, rank) in enumerate(zip(chosen[g], ranks_of(chosen[g], sources))):
            column = (groups * heads + 1) * width + 3 * g + j
            out_ref[:, column : column + 1] = (block * capacity + rank).astype(jnp.float32)
        keys = k_ref[:, g * width : (g + 1) * width]
        values = v_ref[:, g * width : (g + 1) * width]
        for h in range(heads):
            at = slice((g * heads + h) * width, (g * heads + h + 1) * width)
            scores = lax.dot_general(
                q_ref[:, at], keys, (((1,), (1,)), ((), ())), preferred_element_type=jnp.float32
            )
            scores = jnp.where(allowed, scores * scale, -jnp.inf)
            highest = jnp.max(scores, axis=1, keepdims=True)
            weights = jnp.exp(scores - highest)
            total = jnp.sum(weights, axis=1, keepdims=True)
            blended = jnp.dot(
                weights.astype(jnp.bfloat16), values, preferred_element_type=jnp.float32
            )
            out_ref[:, at] = blended / total
            column = groups * heads * width + g * heads + h
            out_ref[:, column : column + 1] = highest + jnp.log(total)


def merge_kernel(first, groups, capacity, heads, width, place_ref, near_ref, back_ref, *refs):
    out_refs, row_ref = refs[:-1], refs[-1]
    tokens = near_ref.shape[0]
    sources = back_ref.shape[0]
    per_source = heads * capacity
    count = out_refs[0].shape[0]
    lanes = back_ref.shape[2]
    row_width = heads * width
    quarter = tokens // len(out_refs)
    extra = back_ref[:, count * per_source :, :].astype(jnp.float32)
    coarse = extra[:, 0, :].astype(jnp.bfloat16)
    fine = extra[:, 1, :].astype(jnp.bfloat16)
    lane = lax.broadcasted_iota(jnp.int32, (lanes, row_width), 0)
    column = lax.broadcasted_iota(jnp.int32, (lanes, row_width), 1)
    spread = ((lane // capacity) % heads == column // width).astype(jnp.float32)
    spread = spread.astype(jnp.bfloat16)
    block_ids = lax.broadcasted_iota(jnp.int32, (tokens, sources), 1)
    slot_ids = lax.broadcasted_iota(jnp.int32, (tokens, sources * capacity), 1)
    lane_ids = lax.broadcasted_iota(jnp.int32, (tokens, lanes), 1)
    for i in range(count):
        g = first + i
        slot_at = (groups * heads + 1) * width + 3 * g
        slots = [near_ref[:, slot_at + j : slot_at + j + 1].astype(jnp.int32) for j in range(3)]
        pick = jnp.concatenate([(slot == slot_ids).astype(jnp.float32) for slot in slots], axis=0)
        block = jnp.concatenate(
            [(slot // capacity == block_ids).astype(jnp.float32) for slot in slots], axis=0
        ).astype(jnp.bfloat16)
        in_group = lane_ids // per_source == i
        rank = jnp.concatenate(
            [
                (in_group & (lane_ids % capacity == slot % capacity)).astype(jnp.float32)
                for slot in slots
            ],
            axis=0,
        )
        rows = back_ref[:, i * per_source : (i + 1) * per_source, :].astype(jnp.float32)
        by_head = [
            rows[:, h * capacity : (h + 1) * capacity, :].reshape(sources * capacity, width)
            for h in range(heads)
        ]
        table = jnp.concatenate(by_head, axis=1).astype(jnp.bfloat16)
        got = jnp.dot(pick.astype(jnp.bfloat16), table, preferred_element_type=jnp.float32)
        lse = jnp.zeros((3 * tokens, row_width), jnp.float32)
        for part in (coarse, fine):
            picked = jnp.dot(block, part, preferred_element_type=jnp.float32)
            picked = (picked * rank).astype(jnp.bfloat16)
            lse += jnp.dot(picked, spread, preferred_element_type=jnp.float32)
        near_lse = jnp.concatenate(
            [
                jnp.broadcast_to(near_ref[:, k : k + 1], (tokens, width))
                for k in range((groups * width + g) * heads, (groups * width + g + 1) * heads)
            ],
            axis=1,
        )
        at = slice(g * row_width, (g + 1) * row_width)
        all_lse = [near_lse] + [lse[j * tokens : (j + 1) * tokens] for j in range(3)]
        all_out = [near_ref[:, at]] + [got[j * tokens : (j + 1) * tokens] for j in range(3)]
        highest = all_lse[0]
        for item in all_lse[1:]:
            highest = jnp.maximum(highest, item)
        top = jnp.zeros((tokens, row_width), jnp.float32)
        bottom = jnp.zeros((tokens, row_width), jnp.float32)
        for item, part in zip(all_lse, all_out):
            weight = jnp.exp(item - highest)
            top += weight * part
            bottom += weight
        row_ref[...] = top / bottom
        for step, out_ref in enumerate(out_refs):
            target = lax.rem(place_ref[0] + step, len(out_refs))
            start = pl.multiple_of(target * quarter, quarter)
            out_ref[i] = row_ref[pl.ds(start, quarter)].astype(jnp.bfloat16)


def assemble_kernel(count, place_ref, *refs):
    piece_refs, out_ref = refs[:-1], refs[-1]
    for i, piece_ref in enumerate(piece_refs):
        origin = lax.rem(place_ref[0] + count - i % count, count)
        first = PARTS[i // count][0]
        out_ref[origin, first : first + piece_ref.shape[0]] = piece_ref[...]


def local(queries, hist_keys, hist_values, own_keys, own_values, choices, positions):
    sources = lax.axis_size("ctx")
    members = lax.axis_size("head")
    tokens, groups, row_width = queries.shape
    keys, _, width = hist_keys.shape
    heads = row_width // width
    capacity = 4 * tokens // sources
    per_source = heads * capacity
    scale = width ** (-0.5)
    quarter = tokens // members
    bf16, f32 = jnp.bfloat16, jnp.float32
    smem = pl.BlockSpec(memory_space=pltpu.SMEM)

    params = pltpu.CompilerParams(vmem_limit_bytes=WIDE_LIMIT)
    small = pltpu.CompilerParams(vmem_limit_bytes=SMALL_LIMIT)

    flat_queries = queries.reshape(tokens, groups * row_width)
    turned = jnp.transpose(choices, (2, 0, 1))

    group = per_source, width
    work = sources * per_source * keys

    def dispatch(first, count):
        return pl.pallas_call(
            lambda *refs: dispatch_kernel(first, sources, capacity, heads, width, *refs),
            out_shape=jax.ShapeDtypeStruct((sources, count) + group, bf16),
            in_specs=[whole()] * 2,
            out_specs=whole(),
            compiler_params=small,
            name="dispatch",
        )(flat_queries, turned)

    sent = [dispatch(*part) for part in PARTS]
    sent[1], hist_keys, hist_values = lax.optimization_barrier((sent[1], hist_keys, hist_values))
    flat_keys = hist_keys.reshape(keys, groups * width)
    flat_values = hist_values.reshape(keys, groups * width)

    def far(received, first, count):
        def held(g):
            return jnp.minimum(g, count - 1)

        block = pl.BlockSpec((keys, width), lambda g: (0, first + held(g)))
        out_rows = count * per_source + LSE_ROWS
        return pl.pallas_call(
            lambda *refs: far_kernel(scale, count, *refs),
            grid=(count + 1,),
            in_specs=[
                pl.BlockSpec((sources, 1) + group, lambda g: (0, held(g), 0, 0)),
                block,
                block,
            ],
            out_specs=pl.BlockSpec((sources,) + group, lambda g: (0, g, 0)),
            out_shape=jax.ShapeDtypeStruct((sources, out_rows, width), bf16),
            scratch_shapes=[
                pltpu.VMEM((sources, width), f32),
                pltpu.VMEM((keys, 2 * width), bf16),
            ],
            compiler_params=params,
            cost_estimate=pl.CostEstimate(
                flops=6 * count * work * width,
                transcendentals=count * work,
                bytes_accessed=4 * keys * count * width,
            ),
            name="far",
        )(received, flat_keys, flat_values)

    received = [lax.all_to_all(item, "ctx", 0, 0, tiled=True) for item in sent]
    parts = [far(item, *part) for item, part in zip(received, PARTS)]
    back = [lax.all_to_all(item, "ctx", 0, 0, tiled=True) for item in parts]

    near = pl.pallas_call(
        lambda *refs: near_kernel(sources, capacity, heads, width, scale, *refs),
        out_shape=jax.ShapeDtypeStruct((tokens, (groups * heads + 2) * width), f32),
        in_specs=[whole()] * 6,
        out_specs=whole(),
        compiler_params=params,
        cost_estimate=pl.CostEstimate(
            flops=4 * tokens * tokens * groups * row_width,
            transcendentals=tokens * tokens * groups * heads,
            bytes_accessed=16 * tokens * groups * row_width,
        ),
        name="near",
    )(
        flat_queries,
        own_keys.reshape(tokens, groups * width),
        own_values.reshape(tokens, groups * width),
        turned,
        positions,
        positions.reshape(tokens, 1),
    )

    place = lax.axis_index("head").astype(jnp.int32).reshape(1)
    pieces = []
    for item, (first, count) in zip(back, PARTS):
        made = pl.pallas_call(
            lambda *refs: merge_kernel(first, groups, capacity, heads, width, *refs),
            out_shape=[jax.ShapeDtypeStruct((count, quarter, row_width), bf16)] * members,
            in_specs=[smem] + [whole()] * 2,
            out_specs=[whole()] * members,
            scratch_shapes=[pltpu.VMEM((tokens, row_width), f32)],
            compiler_params=small,
            name="merge",
        )(place, near, item)
        made = list(made)
        for step in ORDER:
            pairs = [(i, (i + step) % members) for i in range(members)]
            made[step] = lax.ppermute(made[step], "head", pairs)
        pieces += made
    joined = pl.pallas_call(
        lambda *refs: assemble_kernel(members, *refs),
        out_shape=jax.ShapeDtypeStruct((members, groups, quarter, row_width), bf16),
        in_specs=[smem] + [whole()] * len(pieces),
        out_specs=whole(),
        compiler_params=small,
        name="assemble",
    )(place, *pieces)
    joined = joined.reshape(members * groups, quarter, row_width)
    return jnp.transpose(joined, (1, 0, 2))


def solution(mesh):
    in_specs = (
        P("ctx", "head", None),
        P("ctx", "head", None),
        P("ctx", "head", None),
        P("ctx", "head", None),
        P("ctx", "head", None),
        P("head", "ctx", None),
        P("ctx", None),
    )
    out_specs = P(("ctx", "head"), None, None)
    return jax.shard_map(local, mesh=mesh, in_specs=in_specs, out_specs=out_specs, check_vma=False)
```

```python
import math

import jax
import jax.numpy as jnp
from jax import lax
from jax.experimental import pallas as pl
from jax.experimental.pallas import tpu as pltpu
from jax.sharding import PartitionSpec as P

PARTS = ((0, 2), (2, 2))
LSE_ROWS = 8
KEY_CHUNK = 256
TILES = 4
ORDER = (2, 1, 3)
WIDE_LIMIT = 60 * 1024 * 1024
SMALL_LIMIT = 24 * 1024 * 1024


def whole():
    return pl.BlockSpec(memory_space=pltpu.VMEM)


def columns_of(choices_ref):
    count, groups, tokens = choices_ref.shape
    rows = choices_ref[...].astype(jnp.float32).reshape(count * groups, tokens)
    pad = jnp.zeros((tokens - count * groups, tokens), jnp.float32)
    columns = jnp.concatenate([rows, pad], axis=0).T.astype(jnp.int32)
    return [[columns[:, j * groups + g : j * groups + g + 1] for j in range(count)] for g in range(groups)]


def ranks_of(chosen, sources):
    tokens = chosen[0].shape[0]
    block_ids = lax.broadcasted_iota(jnp.int32, (tokens, sources), 1)
    hits = [(item == block_ids).astype(jnp.float32) for item in chosen]
    occupied = (hits[0] + hits[1] + hits[2]).astype(jnp.bfloat16)
    row = lax.broadcasted_iota(jnp.int32, (tokens, tokens), 0)
    column = lax.broadcasted_iota(jnp.int32, (tokens, tokens), 1)
    before = (column < row).astype(jnp.bfloat16)
    earlier = jnp.dot(before, occupied, preferred_element_type=jnp.float32)
    return [jnp.sum(hit * earlier, axis=1, keepdims=True).astype(jnp.int32) for hit in hits]


def fill_slots(picked, rows, sources, capacity, heads, width):
    pick = picked.astype(jnp.float32).T.astype(jnp.bfloat16)
    filled = jnp.dot(pick, rows, preferred_element_type=jnp.float32)
    filled = filled.reshape(sources, capacity, heads * width)
    by_head = [filled[:, :, h * width : (h + 1) * width] for h in range(heads)]
    return jnp.concatenate(by_head, axis=1).astype(jnp.bfloat16)


def dispatch_kernel(first, sources, capacity, heads, width, q_ref, choices_ref, out_ref):
    tokens = choices_ref.shape[2]
    row_width = heads * width
    chosen = columns_of(choices_ref)
    slot_ids = lax.broadcasted_iota(jnp.int32, (tokens, sources * capacity), 1)
    for i in range(out_ref.shape[1]):
        g = first + i
        hit = None
        for block, rank in zip(chosen[g], ranks_of(chosen[g], sources)):
            mine = block * capacity + rank == slot_ids
            hit = mine if hit is None else hit | mine
        rows = q_ref[:, g * row_width : (g + 1) * row_width]
        out_ref[:, i] = fill_slots(hit, rows, sources, capacity, heads, width)


def far_group(scale, slot, q_ref, k_ref, v_ref, out_ref, lse_ref, wide_ref):
    sources, _, per_source, width = q_ref.shape
    keys = k_ref.shape[0]
    wide_ref[:, :width] = v_ref[...]
    wide_ref[:, width:] = jnp.ones((keys, width), jnp.bfloat16)
    fold = scale * math.log2(math.e)
    deep = sources // TILES
    rows = deep * per_source
    shape = (deep, per_source, width)
    lane = lax.broadcasted_iota(jnp.int32, shape, 2)
    index = lax.broadcasted_iota(jnp.int32, shape, 1)
    mine = lane == index + slot * per_source
    for tile in range(TILES):
        here = slice(tile * deep, (tile + 1) * deep)
        q = q_ref[here, 0].reshape(rows, width)
        highest = None
        for start in range(0, keys, KEY_CHUNK):
            scores = lax.dot_general(
                q,
                k_ref[start : start + KEY_CHUNK],
                (((1,), (1,)), ((), ())),
                preferred_element_type=jnp.float32,
            )
            top = jnp.max(scores, axis=1, keepdims=True)
            top = top if highest is None else jnp.maximum(highest, top)
            weights = jnp.exp2((scores - top) * fold).astype(jnp.bfloat16)
            part = jnp.dot(
                weights, wide_ref[start : start + KEY_CHUNK], preferred_element_type=jnp.float32
            )
            both = part if highest is None else both * jnp.exp2((highest - top) * fold) + part
            highest = top
        total = both[:, width:]
        blended = both[:, :width] / total
        lse = (highest * scale + jnp.log(total)).reshape(shape)
        out_ref[here] = blended.astype(jnp.bfloat16).reshape(shape)
        lse_ref[here] += jnp.sum(jnp.where(mine, lse, 0.0), axis=1)


def far_kernel(scale, groups, q_ref, k_ref, v_ref, out_ref, lse_ref, wide_ref):
    g = pl.program_id(0)
    sources, width = q_ref.shape[0], k_ref.shape[1]

    @pl.when(g == 0)
    def _():
        lse_ref[...] = jnp.zeros_like(lse_ref)

    @pl.when(g < groups)
    def _():
        far_group(scale, g, q_ref, k_ref, v_ref, out_ref, lse_ref, wide_ref)

    @pl.when(g == groups)
    def _():
        table = lse_ref[...]
        coarse = table.astype(jnp.bfloat16).astype(jnp.float32)
        rest = jnp.zeros((sources, out_ref.shape[1] - 2, width), jnp.float32)
        extra = jnp.concatenate([coarse[:, None, :], (table - coarse)[:, None, :], rest], axis=1)
        out_ref[...] = extra.astype(jnp.bfloat16)


def near_kernel(sources, capacity, heads, width, scale, q_ref, k_ref, v_ref, choices_ref,
                row_pos_ref, col_pos_ref, out_ref):
    groups, tokens = choices_ref.shape[1:]
    allowed = row_pos_ref[...] <= col_pos_ref[...]
    chosen = columns_of(choices_ref)
    for g in range(groups):
        for j, (block, rank) in enumerate(zip(chosen[g], ranks_of(chosen[g], sources))):
            column = (groups * heads + 1) * width + 3 * g + j
            out_ref[:, column : column + 1] = (block * capacity + rank).astype(jnp.float32)
        keys = k_ref[:, g * width : (g + 1) * width]
        values = v_ref[:, g * width : (g + 1) * width]
        for h in range(heads):
            at = slice((g * heads + h) * width, (g * heads + h + 1) * width)
            scores = lax.dot_general(
                q_ref[:, at], keys, (((1,), (1,)), ((), ())), preferred_element_type=jnp.float32
            )
            scores = jnp.where(allowed, scores * scale, -jnp.inf)
            highest = jnp.max(scores, axis=1, keepdims=True)
            weights = jnp.exp(scores - highest)
            total = jnp.sum(weights, axis=1, keepdims=True)
            blended = jnp.dot(
                weights.astype(jnp.bfloat16), values, preferred_element_type=jnp.float32
            )
            out_ref[:, at] = blended / total
            column = groups * heads * width + g * heads + h
            out_ref[:, column : column + 1] = highest + jnp.log(total)


def merge_kernel(first, groups, capacity, heads, width, place_ref, near_ref, back_ref, *refs):
    out_refs, row_ref = refs[:-1], refs[-1]
    tokens = near_ref.shape[0]
    sources = back_ref.shape[0]
    per_source = heads * capacity
    count = out_refs[0].shape[0]
    lanes = back_ref.shape[2]
    row_width = heads * width
    quarter = tokens // len(out_refs)
    extra = back_ref[:, count * per_source :, :].astype(jnp.float32)
    coarse = extra[:, 0, :].astype(jnp.bfloat16)
    fine = extra[:, 1, :].astype(jnp.bfloat16)
    lane = lax.broadcasted_iota(jnp.int32, (lanes, row_width), 0)
    column = lax.broadcasted_iota(jnp.int32, (lanes, row_width), 1)
    spread = ((lane // capacity) % heads == column // width).astype(jnp.float32)
    spread = spread.astype(jnp.bfloat16)
    block_ids = lax.broadcasted_iota(jnp.int32, (tokens, sources), 1)
    slot_ids = lax.broadcasted_iota(jnp.int32, (tokens, sources * capacity), 1)
    lane_ids = lax.broadcasted_iota(jnp.int32, (tokens, lanes), 1)
    for i in range(count):
        g = first + i
        slot_at = (groups * heads + 1) * width + 3 * g
        slots = [near_ref[:, slot_at + j : slot_at + j + 1].astype(jnp.int32) for j in range(3)]
        pick = jnp.concatenate([(slot == slot_ids).astype(jnp.float32) for slot in slots], axis=0)
        block = jnp.concatenate(
            [(slot // capacity == block_ids).astype(jnp.float32) for slot in slots], axis=0
        ).astype(jnp.bfloat16)
        in_group = lane_ids // per_source == i
        rank = jnp.concatenate(
            [
                (in_group & (lane_ids % capacity == slot % capacity)).astype(jnp.float32)
                for slot in slots
            ],
            axis=0,
        )
        rows = back_ref[:, i * per_source : (i + 1) * per_source, :].astype(jnp.float32)
        by_head = [
            rows[:, h * capacity : (h + 1) * capacity, :].reshape(sources * capacity, width)
            for h in range(heads)
        ]
        table = jnp.concatenate(by_head, axis=1).astype(jnp.bfloat16)
        got = jnp.dot(pick.astype(jnp.bfloat16), table, preferred_element_type=jnp.float32)
        lse = jnp.zeros((3 * tokens, row_width), jnp.float32)
        for part in (coarse, fine):
            picked = jnp.dot(block, part, preferred_element_type=jnp.float32)
            picked = (picked * rank).astype(jnp.bfloat16)
            lse += jnp.dot(picked, spread, preferred_element_type=jnp.float32)
        near_lse = jnp.concatenate(
            [
                jnp.broadcast_to(near_ref[:, k : k + 1], (tokens, width))
                for k in range((groups * width + g) * heads, (groups * width + g + 1) * heads)
            ],
            axis=1,
        )
        at = slice(g * row_width, (g + 1) * row_width)
        all_lse = [near_lse] + [lse[j * tokens : (j + 1) * tokens] for j in range(3)]
        all_out = [near_ref[:, at]] + [got[j * tokens : (j + 1) * tokens] for j in range(3)]
        highest = all_lse[0]
        for item in all_lse[1:]:
            highest = jnp.maximum(highest, item)
        top = jnp.zeros((tokens, row_width), jnp.float32)
        bottom = jnp.zeros((tokens, row_width), jnp.float32)
        for item, part in zip(all_lse, all_out):
            weight = jnp.exp(item - highest)
            top += weight * part
            bottom += weight
        row_ref[...] = top / bottom
        for step, out_ref in enumerate(out_refs):
            target = lax.rem(place_ref[0] + step, len(out_refs))
            start = pl.multiple_of(target * quarter, quarter)
            out_ref[i] = row_ref[pl.ds(start, quarter)].astype(jnp.bfloat16)


def assemble_kernel(count, place_ref, *refs):
    piece_refs, out_ref, row_ref = refs[:-2], refs[-2], refs[-1]
    groups = row_ref.shape[0] // count
    for i, piece_ref in enumerate(piece_refs):
        origin = lax.rem(place_ref[0] + count - i % count, count)
        first = origin * groups + PARTS[i // count][0]
        row_ref[pl.ds(first, piece_ref.shape[0])] = piece_ref[...].astype(jnp.float32)
    out_ref[...] = jnp.swapaxes(row_ref[...], 0, 1).astype(out_ref.dtype)


def local(queries, hist_keys, hist_values, own_keys, own_values, choices, positions):
    sources = lax.axis_size("ctx")
    members = lax.axis_size("head")
    tokens, groups, row_width = queries.shape
    keys, _, width = hist_keys.shape
    heads = row_width // width
    capacity = 4 * tokens // sources
    per_source = heads * capacity
    scale = width ** (-0.5)
    quarter = tokens // members
    bf16, f32 = jnp.bfloat16, jnp.float32
    smem = pl.BlockSpec(memory_space=pltpu.SMEM)

    params = pltpu.CompilerParams(vmem_limit_bytes=WIDE_LIMIT)
    small = pltpu.CompilerParams(vmem_limit_bytes=SMALL_LIMIT)

    flat_queries = queries.reshape(tokens, groups * row_width)
    turned = jnp.transpose(choices, (2, 0, 1))

    group = per_source, width
    work = sources * per_source * keys

    def dispatch(first, count):
        return pl.pallas_call(
            lambda *refs: dispatch_kernel(first, sources, capacity, heads, width, *refs),
            out_shape=jax.ShapeDtypeStruct((sources, count) + group, bf16),
            in_specs=[whole()] * 2,
            out_specs=whole(),
            compiler_params=small,
            name="dispatch",
        )(flat_queries, turned)

    sent = [dispatch(*part) for part in PARTS]
    sent[1], hist_keys, hist_values = lax.optimization_barrier((sent[1], hist_keys, hist_values))
    flat_keys = hist_keys.reshape(keys, groups * width)
    flat_values = hist_values.reshape(keys, groups * width)

    def far(received, first, count):
        def held(g):
            return jnp.minimum(g, count - 1)

        block = pl.BlockSpec((keys, width), lambda g: (0, first + held(g)))
        out_rows = count * per_source + LSE_ROWS
        return pl.pallas_call(
            lambda *refs: far_kernel(scale, count, *refs),
            grid=(count + 1,),
            in_specs=[
                pl.BlockSpec((sources, 1) + group, lambda g: (0, held(g), 0, 0)),
                block,
                block,
            ],
            out_specs=pl.BlockSpec((sources,) + group, lambda g: (0, g, 0)),
            out_shape=jax.ShapeDtypeStruct((sources, out_rows, width), bf16),
            scratch_shapes=[
                pltpu.VMEM((sources, width), f32),
                pltpu.VMEM((keys, 2 * width), bf16),
            ],
            compiler_params=params,
            cost_estimate=pl.CostEstimate(
                flops=6 * count * work * width,
                transcendentals=count * work,
                bytes_accessed=4 * keys * count * width,
            ),
            name="far",
        )(received, flat_keys, flat_values)

    received = [lax.all_to_all(item, "ctx", 0, 0, tiled=True) for item in sent]
    parts = [far(item, *part) for item, part in zip(received, PARTS)]
    rows = PARTS[0][1] * per_source + LSE_ROWS // 2
    parts[0] = parts[0][:, :rows].reshape(sources, rows // 4, 4, width)
    back = [lax.all_to_all(item, "ctx", 0, 0, tiled=True) for item in parts]
    back[0] = back[0].reshape(sources, rows, width)

    near = pl.pallas_call(
        lambda *refs: near_kernel(sources, capacity, heads, width, scale, *refs),
        out_shape=jax.ShapeDtypeStruct((tokens, (groups * heads + 2) * width), f32),
        in_specs=[whole()] * 6,
        out_specs=whole(),
        compiler_params=params,
        cost_estimate=pl.CostEstimate(
            flops=4 * tokens * tokens * groups * row_width,
            transcendentals=tokens * tokens * groups * heads,
            bytes_accessed=16 * tokens * groups * row_width,
        ),
        name="near",
    )(
        flat_queries,
        own_keys.reshape(tokens, groups * width),
        own_values.reshape(tokens, groups * width),
        turned,
        positions,
        positions.reshape(tokens, 1),
    )

    place = lax.axis_index("head").astype(jnp.int32).reshape(1)
    pieces = []
    for item, (first, count) in zip(back, PARTS):
        made = pl.pallas_call(
            lambda *refs: merge_kernel(first, groups, capacity, heads, width, *refs),
            out_shape=[jax.ShapeDtypeStruct((count, quarter, row_width), bf16)] * members,
            in_specs=[smem] + [whole()] * 2,
            out_specs=[whole()] * members,
            scratch_shapes=[pltpu.VMEM((tokens, row_width), f32)],
            compiler_params=small,
            name="merge",
        )(place, near, item)
        made = list(made)
        for step in ORDER:
            pairs = [(i, (i + step) % members) for i in range(members)]
            made[step] = lax.ppermute(made[step], "head", pairs)
        pieces += made
    return pl.pallas_call(
        lambda *refs: assemble_kernel(members, *refs),
        out_shape=jax.ShapeDtypeStruct((quarter, members * groups, row_width), bf16),
        in_specs=[smem] + [whole()] * len(pieces),
        out_specs=whole(),
        scratch_shapes=[pltpu.VMEM((members * groups, quarter, row_width), f32)],
        compiler_params=small,
        name="assemble",
    )(place, *pieces)


def solution(mesh):
    in_specs = (
        P("ctx", "head", None),
        P("ctx", "head", None),
        P("ctx", "head", None),
        P("ctx", "head", None),
        P("ctx", "head", None),
        P("head", "ctx", None),
        P("ctx", None),
    )
    out_specs = P(("ctx", "head"), None, None)
    return jax.shard_map(local, mesh=mesh, in_specs=in_specs, out_specs=out_specs, check_vma=False)
```

```python
import math

import jax
import jax.numpy as jnp
from jax import lax
from jax.experimental import pallas as pl
from jax.experimental.pallas import tpu as pltpu
from jax.sharding import PartitionSpec as P

PARTS = ((0, 2), (2, 2))
LSE_ROWS = 8
KEY_CHUNK = 256
TILES = 4
ORDER = (2, 1, 3)
WIDE_LIMIT = 60 * 1024 * 1024
SMALL_LIMIT = 24 * 1024 * 1024


def whole():
    return pl.BlockSpec(memory_space=pltpu.VMEM)


def columns_of(choices_ref):
    count, groups, tokens = choices_ref.shape
    rows = choices_ref[...].astype(jnp.float32).reshape(count * groups, tokens)
    pad = jnp.zeros((tokens - count * groups, tokens), jnp.float32)
    columns = jnp.concatenate([rows, pad], axis=0).T.astype(jnp.int32)
    return [[columns[:, j * groups + g : j * groups + g + 1] for j in range(count)] for g in range(groups)]


def ranks_of(chosen, sources):
    tokens = chosen[0].shape[0]
    block_ids = lax.broadcasted_iota(jnp.int32, (tokens, sources), 1)
    hits = [(item == block_ids).astype(jnp.float32) for item in chosen]
    occupied = (hits[0] + hits[1] + hits[2]).astype(jnp.bfloat16)
    row = lax.broadcasted_iota(jnp.int32, (tokens, tokens), 0)
    column = lax.broadcasted_iota(jnp.int32, (tokens, tokens), 1)
    before = (column < row).astype(jnp.bfloat16)
    earlier = jnp.dot(before, occupied, preferred_element_type=jnp.float32)
    return [jnp.sum(hit * earlier, axis=1, keepdims=True).astype(jnp.int32) for hit in hits]


def fill_slots(picked, rows, sources, capacity, heads, width):
    pick = picked.astype(jnp.float32).T.astype(jnp.bfloat16)
    filled = jnp.dot(pick, rows, preferred_element_type=jnp.float32)
    filled = filled.reshape(sources, capacity, heads * width)
    by_head = [filled[:, :, h * width : (h + 1) * width] for h in range(heads)]
    return jnp.concatenate(by_head, axis=1).astype(jnp.bfloat16)


def dispatch_kernel(first, sources, capacity, heads, width, q_ref, choices_ref, out_ref):
    tokens = choices_ref.shape[2]
    row_width = heads * width
    chosen = columns_of(choices_ref)
    slot_ids = lax.broadcasted_iota(jnp.int32, (tokens, sources * capacity), 1)
    for i in range(out_ref.shape[1]):
        g = first + i
        hit = None
        for block, rank in zip(chosen[g], ranks_of(chosen[g], sources)):
            mine = block * capacity + rank == slot_ids
            hit = mine if hit is None else hit | mine
        rows = q_ref[:, g * row_width : (g + 1) * row_width]
        out_ref[:, i] = fill_slots(hit, rows, sources, capacity, heads, width)


def far_group(scale, slot, q_ref, k_ref, v_ref, out_ref, lse_ref, wide_ref):
    sources, _, per_source, width = q_ref.shape
    keys = k_ref.shape[0]
    wide_ref[:, :width] = v_ref[...]
    wide_ref[:, width:] = jnp.ones((keys, width), jnp.bfloat16)
    fold = scale * math.log2(math.e)
    deep = sources // TILES
    rows = deep * per_source
    shape = (deep, per_source, width)
    lane = lax.broadcasted_iota(jnp.int32, shape, 2)
    index = lax.broadcasted_iota(jnp.int32, shape, 1)
    mine = lane == index + slot * per_source
    for tile in range(TILES):
        here = slice(tile * deep, (tile + 1) * deep)
        q = q_ref[here, 0].reshape(rows, width)
        highest = None
        for start in range(0, keys, KEY_CHUNK):
            scores = lax.dot_general(
                q,
                k_ref[start : start + KEY_CHUNK],
                (((1,), (1,)), ((), ())),
                preferred_element_type=jnp.float32,
            )
            top = jnp.max(scores, axis=1, keepdims=True)
            top = top if highest is None else jnp.maximum(highest, top)
            weights = jnp.exp2((scores - top) * fold).astype(jnp.bfloat16)
            part = jnp.dot(
                weights, wide_ref[start : start + KEY_CHUNK], preferred_element_type=jnp.float32
            )
            both = part if highest is None else both * jnp.exp2((highest - top) * fold) + part
            highest = top
        total = both[:, width:]
        blended = both[:, :width] / total
        lse = (highest * scale + jnp.log(total)).reshape(shape)
        out_ref[here] = blended.astype(jnp.bfloat16).reshape(shape)
        lse_ref[here] += jnp.sum(jnp.where(mine, lse, 0.0), axis=1)


def far_kernel(scale, groups, q_ref, k_ref, v_ref, out_ref, lse_ref, wide_ref):
    g = pl.program_id(0)
    sources, width = q_ref.shape[0], k_ref.shape[1]

    @pl.when(g == 0)
    def _():
        lse_ref[...] = jnp.zeros_like(lse_ref)

    @pl.when(g < groups)
    def _():
        far_group(scale, g, q_ref, k_ref, v_ref, out_ref, lse_ref, wide_ref)

    @pl.when(g == groups)
    def _():
        table = lse_ref[...]
        coarse = table.astype(jnp.bfloat16).astype(jnp.float32)
        rest = jnp.zeros((sources, out_ref.shape[1] - 2, width), jnp.float32)
        extra = jnp.concatenate([coarse[:, None, :], (table - coarse)[:, None, :], rest], axis=1)
        out_ref[...] = extra.astype(jnp.bfloat16)


def near_kernel(sources, capacity, heads, width, scale, q_ref, k_ref, v_ref, choices_ref,
                row_pos_ref, col_pos_ref, out_ref):
    groups, tokens = choices_ref.shape[1:]
    allowed = row_pos_ref[...] <= col_pos_ref[...]
    chosen = columns_of(choices_ref)
    for g in range(groups):
        for j, (block, rank) in enumerate(zip(chosen[g], ranks_of(chosen[g], sources))):
            column = (groups * heads + 1) * width + 3 * g + j
            out_ref[:, column : column + 1] = (block * capacity + rank).astype(jnp.float32)
        keys = k_ref[:, g * width : (g + 1) * width]
        values = v_ref[:, g * width : (g + 1) * width]
        for h in range(heads):
            at = slice((g * heads + h) * width, (g * heads + h + 1) * width)
            scores = lax.dot_general(
                q_ref[:, at], keys, (((1,), (1,)), ((), ())), preferred_element_type=jnp.float32
            )
            scores = jnp.where(allowed, scores * scale, -jnp.inf)
            highest = jnp.max(scores, axis=1, keepdims=True)
            weights = jnp.exp(scores - highest)
            total = jnp.sum(weights, axis=1, keepdims=True)
            blended = jnp.dot(
                weights.astype(jnp.bfloat16), values, preferred_element_type=jnp.float32
            )
            out_ref[:, at] = blended / total
            column = groups * heads * width + g * heads + h
            out_ref[:, column : column + 1] = highest + jnp.log(total)


def merge_kernel(first, groups, capacity, heads, width, place_ref, near_ref, back_ref, *refs):
    out_refs, row_ref = refs[:-1], refs[-1]
    tokens = near_ref.shape[0]
    sources = back_ref.shape[0]
    per_source = heads * capacity
    count = out_refs[0].shape[0]
    lanes = back_ref.shape[2]
    row_width = heads * width
    quarter = tokens // len(out_refs)
    extra = back_ref[:, count * per_source :, :].astype(jnp.float32)
    coarse = extra[:, 0, :].astype(jnp.bfloat16)
    fine = extra[:, 1, :].astype(jnp.bfloat16)
    lane = lax.broadcasted_iota(jnp.int32, (lanes, row_width), 0)
    column = lax.broadcasted_iota(jnp.int32, (lanes, row_width), 1)
    spread = ((lane // capacity) % heads == column // width).astype(jnp.float32)
    spread = spread.astype(jnp.bfloat16)
    block_ids = lax.broadcasted_iota(jnp.int32, (tokens, sources), 1)
    slot_ids = lax.broadcasted_iota(jnp.int32, (tokens, sources * capacity), 1)
    lane_ids = lax.broadcasted_iota(jnp.int32, (tokens, lanes), 1)
    for i in range(count):
        g = first + i
        slot_at = (groups * heads + 1) * width + 3 * g
        slots = [near_ref[:, slot_at + j : slot_at + j + 1].astype(jnp.int32) for j in range(3)]
        pick = jnp.concatenate([(slot == slot_ids).astype(jnp.float32) for slot in slots], axis=0)
        block = jnp.concatenate(
            [(slot // capacity == block_ids).astype(jnp.float32) for slot in slots], axis=0
        ).astype(jnp.bfloat16)
        in_group = lane_ids // per_source == i
        rank = jnp.concatenate(
            [
                (in_group & (lane_ids % capacity == slot % capacity)).astype(jnp.float32)
                for slot in slots
            ],
            axis=0,
        )
        rows = back_ref[:, i * per_source : (i + 1) * per_source, :].astype(jnp.float32)
        by_head = [
            rows[:, h * capacity : (h + 1) * capacity, :].reshape(sources * capacity, width)
            for h in range(heads)
        ]
        table = jnp.concatenate(by_head, axis=1).astype(jnp.bfloat16)
        got = jnp.dot(pick.astype(jnp.bfloat16), table, preferred_element_type=jnp.float32)
        lse = jnp.zeros((3 * tokens, row_width), jnp.float32)
        for part in (coarse, fine):
            picked = jnp.dot(block, part, preferred_element_type=jnp.float32)
            picked = (picked * rank).astype(jnp.bfloat16)
            lse += jnp.dot(picked, spread, preferred_element_type=jnp.float32)
        near_lse = jnp.concatenate(
            [
                jnp.broadcast_to(near_ref[:, k : k + 1], (tokens, width))
                for k in range((groups * width + g) * heads, (groups * width + g + 1) * heads)
            ],
            axis=1,
        )
        at = slice(g * row_width, (g + 1) * row_width)
        all_lse = [near_lse] + [lse[j * tokens : (j + 1) * tokens] for j in range(3)]
        all_out = [near_ref[:, at]] + [got[j * tokens : (j + 1) * tokens] for j in range(3)]
        highest = all_lse[0]
        for item in all_lse[1:]:
            highest = jnp.maximum(highest, item)
        top = jnp.zeros((tokens, row_width), jnp.float32)
        bottom = jnp.zeros((tokens, row_width), jnp.float32)
        for item, part in zip(all_lse, all_out):
            weight = jnp.exp(item - highest)
            top += weight * part
            bottom += weight
        row_ref[...] = top / bottom
        for step, out_ref in enumerate(out_refs):
            target = lax.rem(place_ref[0] + step, len(out_refs))
            start = pl.multiple_of(target * quarter, quarter)
            out_ref[i] = row_ref[pl.ds(start, quarter)].astype(jnp.bfloat16)


def assemble_kernel(count, place_ref, *refs):
    piece_refs, out_ref, row_ref = refs[:-2], refs[-2], refs[-1]
    groups = row_ref.shape[0] // count
    for i, piece_ref in enumerate(piece_refs):
        origin = lax.rem(place_ref[0] + count - i % count, count)
        first = origin * groups + PARTS[i // count][0]
        row_ref[pl.ds(first, piece_ref.shape[0])] = piece_ref[...].astype(jnp.float32)
    out_ref[...] = jnp.swapaxes(row_ref[...], 0, 1).astype(out_ref.dtype)


def local(queries, hist_keys, hist_values, own_keys, own_values, choices, positions):
    sources = lax.axis_size("ctx")
    members = lax.axis_size("head")
    tokens, groups, row_width = queries.shape
    keys, _, width = hist_keys.shape
    heads = row_width // width
    capacity = 4 * tokens // sources
    per_source = heads * capacity
    scale = width ** (-0.5)
    quarter = tokens // members
    bf16, f32 = jnp.bfloat16, jnp.float32
    smem = pl.BlockSpec(memory_space=pltpu.SMEM)

    params = pltpu.CompilerParams(vmem_limit_bytes=WIDE_LIMIT)
    small = pltpu.CompilerParams(vmem_limit_bytes=SMALL_LIMIT)

    flat_queries = queries.reshape(tokens, groups * row_width)
    turned = jnp.transpose(choices, (2, 0, 1))

    group = per_source, width
    work = sources * per_source * keys

    def dispatch(first, count):
        return pl.pallas_call(
            lambda *refs: dispatch_kernel(first, sources, capacity, heads, width, *refs),
            out_shape=jax.ShapeDtypeStruct((sources, count) + group, bf16),
            in_specs=[whole()] * 2,
            out_specs=whole(),
            compiler_params=params if first else small,
            name="dispatch",
        )(flat_queries, turned)

    sent = [dispatch(*part) for part in PARTS]
    sent[1], hist_keys, hist_values = lax.optimization_barrier((sent[1], hist_keys, hist_values))
    flat_keys = hist_keys.reshape(keys, groups * width)
    flat_values = hist_values.reshape(keys, groups * width)

    def far(received, first, count):
        def held(g):
            return jnp.minimum(g, count - 1)

        block = pl.BlockSpec((keys, width), lambda g: (0, first + held(g)))
        out_rows = count * per_source + LSE_ROWS
        return pl.pallas_call(
            lambda *refs: far_kernel(scale, count, *refs),
            grid=(count + 1,),
            in_specs=[
                pl.BlockSpec((sources, 1) + group, lambda g: (0, held(g), 0, 0)),
                block,
                block,
            ],
            out_specs=pl.BlockSpec((sources,) + group, lambda g: (0, g, 0)),
            out_shape=jax.ShapeDtypeStruct((sources, out_rows, width), bf16),
            scratch_shapes=[
                pltpu.VMEM((sources, width), f32),
                pltpu.VMEM((keys, 2 * width), bf16),
            ],
            compiler_params=params,
            cost_estimate=pl.CostEstimate(
                flops=6 * count * work * width,
                transcendentals=count * work,
                bytes_accessed=4 * keys * count * width,
            ),
            name="far",
        )(received, flat_keys, flat_values)

    received = [lax.all_to_all(item, "ctx", 0, 0, tiled=True) for item in sent]
    parts = [far(item, *part) for item, part in zip(received, PARTS)]
    rows = PARTS[0][1] * per_source + LSE_ROWS // 2
    parts[0] = parts[0][:, :rows].reshape(sources, rows // 4, 4, width)
    back = [lax.all_to_all(item, "ctx", 0, 0, tiled=True) for item in parts]
    back[0] = back[0].reshape(sources, rows, width)

    near = pl.pallas_call(
        lambda *refs: near_kernel(sources, capacity, heads, width, scale, *refs),
        out_shape=jax.ShapeDtypeStruct((tokens, (groups * heads + 2) * width), f32),
        in_specs=[whole()] * 6,
        out_specs=whole(),
        compiler_params=params,
        cost_estimate=pl.CostEstimate(
            flops=4 * tokens * tokens * groups * row_width,
            transcendentals=tokens * tokens * groups * heads,
            bytes_accessed=16 * tokens * groups * row_width,
        ),
        name="near",
    )(
        flat_queries,
        own_keys.reshape(tokens, groups * width),
        own_values.reshape(tokens, groups * width),
        turned,
        positions,
        positions.reshape(tokens, 1),
    )

    place = lax.axis_index("head").astype(jnp.int32).reshape(1)
    pieces = []
    for item, (first, count) in zip(back, PARTS):
        made = pl.pallas_call(
            lambda *refs: merge_kernel(first, groups, capacity, heads, width, *refs),
            out_shape=[jax.ShapeDtypeStruct((count, quarter, row_width), bf16)] * members,
            in_specs=[smem] + [whole()] * 2,
            out_specs=[whole()] * members,
            scratch_shapes=[pltpu.VMEM((tokens, row_width), f32)],
            compiler_params=small,
            name="merge",
        )(place, near, item)
        made = list(made)
        for step in ORDER:
            pairs = [(i, (i + step) % members) for i in range(members)]
            made[step] = lax.ppermute(made[step], "head", pairs)
        pieces += made
    return pl.pallas_call(
        lambda *refs: assemble_kernel(members, *refs),
        out_shape=jax.ShapeDtypeStruct((quarter, members * groups, row_width), bf16),
        in_specs=[smem] + [whole()] * len(pieces),
        out_specs=whole(),
        scratch_shapes=[pltpu.VMEM((members * groups, quarter, row_width), f32)],
        compiler_params=small,
        name="assemble",
    )(place, *pieces)


def solution(mesh):
    in_specs = (
        P("ctx", "head", None),
        P("ctx", "head", None),
        P("ctx", "head", None),
        P("ctx", "head", None),
        P("ctx", "head", None),
        P("head", "ctx", None),
        P("ctx", None),
    )
    out_specs = P(("ctx", "head"), None, None)
    return jax.shard_map(local, mesh=mesh, in_specs=in_specs, out_specs=out_specs, check_vma=False)
```
